256 devices in a mesh: fsdp: 16 (over z, core), seq: 16 (over x, y).
Axes of the slice: x: 4, y: 4, z: 8, core: 2. Of those that a mesh axis runs over, the one named last changes fastest.
Arguments:
- tokens: bfloat16 [16, 7680, 1536], P('fsdp', 'seq'), may hold values from -9.5 to 9.5
- assignment: int32 [16, 7680], P('fsdp', 'seq'), may hold values from 0 to 15, as said below
- w_query: bfloat16 [1536, 768], P('fsdp'), may hold values from -0.15625 to 0.15625
- w_value: bfloat16 [1536, 768], P('fsdp'), may hold values from -0.15625 to 0.15625
- out_grad: bfloat16 [16, 7680, 768], P('fsdp', 'seq'), may hold values from -6 to 6
Outputs:
- attn_out: bfloat16 [16, 7680, 768], P('fsdp', 'seq')
- tokens_grad: bfloat16 [16, 7680, 1536], P('fsdp', 'seq')
- grad_wq: float32 [1536, 768], P('fsdp', 'seq')
- grad_wv: float32 [1536, 768], P('fsdp', 'seq')
The draws below stay inside these ranges and needn't reach their ends.
Inputs may be any that keep to these rules, and one draw needn't show every extreme that they name: `assignment`: cluster c of a sequence is owned by index c of seq. Every cluster holds exactly 480 tokens of its sequence. Of the tokens one device holds, at most 46 fall into one cluster, and some device of every sequence reaches 46.
All inputs are finite; a program needn't handle non-finite values.
Results may differ from the reference program's by a relative error of at most 0.028.
Values may be sent and summed in bfloat16 or wider, within the bound.
No kernel may reach another device: no remote copies, remote signals or barrier semaphores. Data moves between devices by JAX's collectives and lax.ppermute only.
A program may use at most 128 MiB of HBM per device.

```python
import jax
import jax.numpy as jnp
from jax import lax

D = 1536
HEADS = 6
HEAD_DIM = 128
CLUSTER = 480
HD = 768
CLUSTERS = 16
SEQ_LEN = 7680
SEQS = 16
PER_PEER = 30
LADDER = 1


def route_one(key):
    count_all = CLUSTERS
    key_ladder, key_turn, key_mixing = jax.random.split(key, 3)
    ladder_order = jax.random.permutation(key_ladder, count_all).astype(jnp.int32)
    indices = jnp.arange(count_all, dtype=jnp.int32)
    ladder = PER_PEER + (2 * indices - (count_all - 1)) * LADDER
    circulant = ladder[ladder_order]
    peak_shift = jnp.argmax(ladder_order).astype(jnp.int32)
    turn = jax.random.randint(key_turn, (), 0, count_all, dtype=jnp.int32)
    plus_minus = jnp.where((indices - peak_shift - 2 * turn) % count_all < count_all // 2, 1, -1).astype(jnp.int32)
    source = indices[:, None]
    target = indices[None, :]
    link_counts = circulant[(target - source) % count_all] + plus_minus[(target + source) % count_all]
    bounds = jnp.cumsum(link_counts, axis=1)
    places = jnp.arange(CLUSTER, dtype=jnp.int32)
    cluster_of = jnp.sum((places[None, :, None] >= bounds[:, None, :]).astype(jnp.int32), axis=2)
    row_keys = jax.random.split(key_mixing, count_all)
    mixed = jax.vmap(lambda row_key, row: row[jax.random.permutation(row_key, CLUSTER)])(row_keys, cluster_of)
    return mixed.reshape(-1).astype(jnp.int32)


def route_all(key):
    seq_keys = jax.random.split(key, SEQS)
    return jax.vmap(route_one)(seq_keys)


def draw_assignment(key, part):
    routes = route_all(key)
    return routes


def draw_tokens(key, part):
    key = jax.random.fold_in(key, 7)
    key_main = jax.random.fold_in(key, 0)
    values = jnp.clip(jax.random.normal(key_main, (SEQS, SEQ_LEN, D), jnp.float32), -6.0, 6.0)
    return values.astype(jnp.bfloat16)


def raised(values, rng, source, target, blocks, factor):
    def block_of(dim):
        return (jnp.arange(values.shape[dim]) // (values.shape[dim] // blocks)).reshape((-1,) + (1,) * (values.ndim - 1 - dim))

    one_side = jax.random.permutation(rng, blocks)[block_of(target)]
    second = (block_of(target) + blocks // 2) % blocks
    return jnp.where((block_of(source) == one_side) | (block_of(source) == second), factor * values, values)


def block_levels(rng, extent, pieces, least, high):
    level = 1.0
    for axis_at, blocks in pieces:
        draws = jax.random.uniform(jax.random.fold_in(jax.random.fold_in(rng, 6), axis_at), (blocks,), jnp.float32, least / len(pieces), high / len(pieces))
        level = level * jnp.repeat(jnp.exp(draws), extent[axis_at] // blocks).reshape((-1,) + (1,) * (len(extent) - 1 - axis_at))
    return level


def scatter_about(rng, dims, deviation, limit, cuts=(), kind=jnp.bfloat16):
    level = block_levels(rng, dims, cuts, -0.22, 0.18) if cuts else 1.0
    values = jax.random.normal(rng, dims, jnp.float32) * deviation * level
    return jnp.minimum(jnp.maximum(values, -limit), limit).astype(kind)


def bell_draw_with(own_key, shape, deviation, reach, shards, heavy, kind=jnp.bfloat16):
    entries = deviation * jax.random.normal(own_key, shape, jnp.float32)
    if shards:
        entries = entries * block_levels(own_key, shape, shards, -0.22, 0.18)
    return jnp.clip(raised(entries, jax.random.fold_in(own_key, 3), *heavy), -reach, reach).astype(kind)


def setup_inputs(seed: int = 0) -> dict:
    seeds = jax.random.split(jax.random.key(seed), 6)
    return {
        "tokens": draw_tokens(jax.random.fold_in(seeds[5], 71), 0),
        "assignment": draw_assignment(jax.random.fold_in(seeds[5], 71), 0),
        "w_query": scatter_about(seeds[2], (D, HD), D ** -0.5, 0.15625, ((0, 16),)),
        "w_value": scatter_about(seeds[3], (D, HD), D ** -0.5, 0.15625, ((0, 16),)),
        "out_grad": bell_draw_with(seeds[4], (SEQS, SEQ_LEN, HD), 1.0, 6.0, ((0, 16), (1, 16)), (1, 2, 16, 2.0)),
    }


def attend_block(queries, values, grads):
    members = queries.shape[0]
    scaling = HEAD_DIM ** -0.5
    query_heads = queries.astype(jnp.float32).reshape(members, HEADS, HEAD_DIM)
    value_heads = values.astype(jnp.float32).reshape(members, HEADS, HEAD_DIM)
    grad_heads = grads.astype(jnp.float32).reshape(members, HEADS, HEAD_DIM)
    scores = jnp.einsum("qhd,khd->hqk", query_heads, query_heads) * scaling
    self_mask = jnp.eye(members, dtype=bool)[None]
    scores = jnp.where(self_mask, -1e30, scores)
    largest = jnp.max(scores, axis=-1, keepdims=True)
    weights = jnp.exp(scores - largest)
    probs = weights / jnp.sum(weights, axis=-1, keepdims=True)
    probs_low = lax.optimization_barrier(probs.astype(jnp.bfloat16)).astype(jnp.float32)
    attended = jnp.einsum("hqk,khd->qhd", probs_low, value_heads).astype(jnp.bfloat16)
    grad_probs = jnp.einsum("qhd,khd->hqk", grad_heads, value_heads)
    grad_values = jnp.einsum("hqk,qhd->khd", probs_low, grad_heads).astype(jnp.bfloat16)
    row_terms = jnp.sum(probs * grad_probs, axis=-1, keepdims=True)
    grad_scores = probs * (grad_probs - row_terms) * scaling
    grad_scores = lax.optimization_barrier(grad_scores.astype(jnp.bfloat16)).astype(jnp.float32)
    grad_queries = jnp.einsum("hqk,khd->qhd", grad_scores, query_heads) + jnp.einsum("hqk,qhd->khd", grad_scores, query_heads)
    grad_queries = grad_queries.astype(jnp.bfloat16)
    return attended.reshape(members, -1), grad_queries.reshape(members, -1), grad_values.reshape(members, -1)


def reference(tokens, assignment, w_query, w_value, out_grad):
    width = w_query.shape[1]

    def one_sequence(carry, inputs):
        features, routes, cotangent = inputs
        queries = jnp.dot(features, w_query, preferred_element_type=jnp.float32).astype(jnp.bfloat16)
        values = jnp.dot(features, w_value, preferred_element_type=jnp.float32).astype(jnp.bfloat16)
        members = jnp.argsort(routes, stable=True).astype(jnp.int32).reshape(CLUSTERS, CLUSTER)
        attended, grad_q, grad_v = lax.map(lambda trio: attend_block(trio[0], trio[1], trio[2]), (queries[members], values[members], cotangent[members]))
        flat = members.reshape(-1)
        attended_home = jnp.zeros((SEQ_LEN, width), jnp.bfloat16).at[flat].set(attended.reshape(-1, width))
        grad_q_home = jnp.zeros((SEQ_LEN, width), jnp.bfloat16).at[flat].set(grad_q.reshape(-1, width))
        grad_v_home = jnp.zeros((SEQ_LEN, width), jnp.bfloat16).at[flat].set(grad_v.reshape(-1, width))
        token_grad = jnp.dot(grad_q_home, w_query.T, preferred_element_type=jnp.float32) + jnp.dot(grad_v_home, w_value.T, preferred_element_type=jnp.float32)
        weight_q = carry[0] + jnp.dot(features.T, grad_q_home, preferred_element_type=jnp.float32)
        weight_v = carry[1] + jnp.dot(features.T, grad_v_home, preferred_element_type=jnp.float32)
        return (weight_q, weight_v), (attended_home, token_grad.astype(jnp.bfloat16))

    start = (jnp.zeros((D, width), jnp.float32), jnp.zeros((D, width), jnp.float32))
    totals, stacked = lax.scan(one_sequence, start, (tokens, assignment, out_grad))
    return stacked[0], stacked[1], totals[0], totals[1]
```

```python
import functools

import jax
import jax.numpy as jnp
from jax import lax
from jax.experimental import pallas as pl
from jax.experimental.pallas import tpu as pltpu
from jax.sharding import PartitionSpec as P

HEAD_DIM = 128
LOG2E = 1.4426950408889634
BF16 = jnp.bfloat16
F32 = jnp.float32
NN = (((1,), (0,)), ((), ()))
NT = (((1,), (1,)), ((), ()))
TN = (((0,), (0,)), ((), ()))
MIB = 1024 * 1024
SLOT = 48
OWNERS = 16
SLOTS = SLOT * OWNERS


def mm(a, b, dims=NN):
    return lax.dot_general(a, b, dims, preferred_element_type=F32)


def iota(shape, dim):
    return lax.broadcasted_iota(jnp.int32, shape, dim)


def vmem():
    return pl.BlockSpec(memory_space=pltpu.VMEM)


def smem():
    return pl.BlockSpec(memory_space=pltpu.SMEM)


def hbm():
    return pl.BlockSpec(memory_space=pl.ANY)


def call(body, outs, ins, args, scratch=(), limit=40, flops=0, moved=0):
    return pl.pallas_call(
        body,
        out_shape=[jax.ShapeDtypeStruct(s, d) for s, d in outs],
        in_specs=ins,
        out_specs=[vmem() for _ in outs],
        scratch_shapes=list(scratch),
        compiler_params=pltpu.CompilerParams(vmem_limit_bytes=limit * MIB),
        cost_estimate=pl.CostEstimate(flops=flops, bytes_accessed=moved, transcendentals=0),
    )(*args)


def pack_body(route_ref, tok_ref, cot_ref, px_ref, pg_ref, slot_ref):
    tok_rows = tok_ref.shape[0]
    route = route_ref[...]
    member = iota((OWNERS, tok_rows), 0) == route
    earlier = (iota((tok_rows, tok_rows), 0) < iota((tok_rows, tok_rows), 1)).astype(BF16)
    before = mm(member.astype(BF16), earlier)
    rank = jnp.sum(jnp.where(member, before, 0.0), axis=0, keepdims=True)
    slot = route * SLOT + rank.astype(jnp.int32)
    slot_ref[...] = slot
    step = 256
    for at in range(0, SLOTS, step):
        row = iota((step, tok_rows), 0) + at
        pick = (row == slot).astype(BF16)
        count = jnp.sum((row == route * SLOT + (SLOT - 1)).astype(F32), axis=1, keepdims=True)
        px_ref[at : at + step] = (mm(pick, tok_ref[...]) + count).astype(BF16)
        pg_ref[at : at + step] = mm(pick, cot_ref[...]).astype(BF16)


def load_weights(ids_ref, block_refs, w_ref, sems):
    rows = block_refs[0].shape[0]
    z = ids_ref[0]
    c = ids_ref[1]
    copies = []
    for n, block in enumerate(block_refs):
        zb = lax.rem(z + (n % 8), 8)
        fb = 2 * zb + (c if n < 8 else 1 - c)
        copies.append(
            pltpu.make_async_copy(
                block, w_ref.at[pl.ds(pl.multiple_of(fb * rows, rows), rows)], sems.at[n]
            )
        )
    return copies


def masked(scores, lo):
    width = scores.shape[1]
    eye = iota((width, width), 0) == iota((width, width), 1)
    parts = [jnp.where(eye, -1e30, scores[lo : lo + width])]
    if lo:
        parts.insert(0, scores[:lo])
    if lo + width < scores.shape[0]:
        parts.append(scores[lo + width :])
    return jnp.concatenate(parts, axis=0) if len(parts) > 1 else parts[0]


def blocks_of(members):
    return [(lo, min(lo + 128, members)) for lo in range(0, members, 128)]


def forward_body(ids_ref, rx_ref, *refs):
    block_refs = refs[:16]
    xc_ref, qv_ref, stat_ref, comp_ref, spread_ref, pa_ref, w_ref, att_ref, sems = refs[16:]
    members, width2 = qv_ref.shape
    width = width2 // 2
    heads = width // HEAD_DIM
    factor = HEAD_DIM ** (-0.5) * LOG2E
    copies = load_weights(ids_ref, block_refs, w_ref, sems)
    for c in copies:
        c.start()
    pick = (iota((OWNERS, SLOTS), 1) == iota((OWNERS, SLOTS), 0) * SLOT + (SLOT - 1)).astype(BF16)
    count = mm(pick, rx_ref[:, 0:128])
    count_t = jnp.transpose(count)[0:8].astype(BF16)
    col = iota((OWNERS, SLOTS), 1)
    first = iota((OWNERS, SLOTS), 0) * SLOT
    past = (col >= first + SLOT).astype(F32)
    inside = ((col >= first) & (col < first + SLOT)).astype(BF16)
    offset = mm(count_t, past.astype(BF16))
    mine = mm(count_t, inside)
    within = iota((8, SLOTS), 1).astype(F32) - SLOT * jnp.sum(past, axis=0, keepdims=True)
    pos = jnp.where(within < mine, offset + within, -1.0)
    pos_row = pos[0:1].astype(jnp.int32)
    pos_col = jnp.transpose(pos)[:, 0:1].astype(jnp.int32)
    comp = (iota((members, SLOTS), 0) == pos_row).astype(BF16)
    comp_ref[...] = comp
    spread_ref[...] = (iota((SLOTS, members), 1) == pos_col).astype(BF16)
    xc_ref[...] = mm(comp, rx_ref[...]).astype(BF16)
    for c in copies:
        c.wait()
    qv_ref[...] = mm(xc_ref[...], w_ref[...]).astype(BF16)

    def head(h, _):
        at = pl.multiple_of(h * HEAD_DIM, HEAD_DIM)
        q = qv_ref[:, pl.ds(at, HEAD_DIM)]
        v_t = jnp.transpose(qv_ref[:, pl.ds(pl.multiple_of(width + at, HEAD_DIM), HEAD_DIM)])
        for lo, hi in blocks_of(members):
            scores = masked(mm(q, q[lo:hi], NT), lo)
            top = jnp.max(scores, axis=0, keepdims=True)
            weights = jnp.exp2((scores - top) * factor)
            inverse = 1.0 / jnp.sum(weights, axis=0, keepdims=True)
            probs = (weights * inverse).astype(BF16)
            out_t = mm(v_t, probs)
            att_ref[lo:hi, pl.ds(at, HEAD_DIM)] = jnp.transpose(out_t).astype(BF16)
            stat_ref[h, 0:1, lo:hi] = top
            stat_ref[h, 1:2, lo:hi] = inverse
        return 0

    lax.fori_loop(0, heads, head, 0)
    pa_ref[...] = mm(spread_ref[...], att_ref[...]).astype(BF16)


def backward_body(ids_ref, rg_ref, qv_ref, stat_ref, comp_ref, gqv_ref, keep_ref, send_ref, gc_ref, p_ref, d_ref):
    members, width2 = qv_ref.shape
    width = width2 // 2
    heads = width // HEAD_DIM
    scaling = HEAD_DIM ** (-0.5)
    factor = scaling * LOG2E
    gc_ref[...] = mm(comp_ref[...], rg_ref[...]).astype(BF16)

    def head(h, _):
        at = pl.multiple_of(h * HEAD_DIM, HEAD_DIM)
        at_v = pl.multiple_of(width + at, HEAD_DIM)
        q = qv_ref[:, pl.ds(at, HEAD_DIM)]
        v = qv_ref[:, pl.ds(at_v, HEAD_DIM)]
        g = gc_ref[:, pl.ds(at, HEAD_DIM)]
        for lo, hi in blocks_of(members):
            scores = masked(mm(q, q[lo:hi], NT), lo)
            top = stat_ref[h, 0:1, lo:hi]
            inverse = stat_ref[h, 1:2, lo:hi]
            probs = jnp.exp2((scores - top) * factor) * inverse
            p_ref[:, lo:hi] = probs.astype(BF16)
            grad_probs = mm(v, g[lo:hi], NT)
            row_terms = jnp.sum(probs * grad_probs, axis=0, keepdims=True)
            d_ref[:, lo:hi] = (probs * (grad_probs - row_terms) * scaling).astype(BF16)
        grad_scores = d_ref[...]
        grad_v = mm(p_ref[...], g)
        grad_q = mm(grad_scores, q) + jnp.transpose(mm(jnp.transpose(q), grad_scores))
        gqv_ref[:, pl.ds(at, HEAD_DIM)] = grad_q.astype(BF16)
        gqv_ref[:, pl.ds(at_v, HEAD_DIM)] = grad_v.astype(BF16)
        return 0

    lax.fori_loop(0, heads, head, 0)

    @pl.when(ids_ref[1] == 0)
    def _():
        keep_ref[...] = gqv_ref[:, :width]
        send_ref[...] = gqv_ref[:, width:]

    @pl.when(ids_ref[1] == 1)
    def _():
        keep_ref[...] = gqv_ref[:, width:]
        send_ref[...] = gqv_ref[:, :width]


def token_grad_body(ids_ref, gqv_ref, spread_ref, *refs):
    block_refs = refs[:16]
    pt_ref, w_ref, sems = refs[16:]
    copies = load_weights(ids_ref, block_refs, w_ref, sems)
    for c in copies:
        c.start()
    for c in copies:
        c.wait()
    grad = mm(gqv_ref[...], w_ref[...], NT).astype(BF16)
    pt_ref[...] = mm(spread_ref[...], grad).astype(BF16)


def weight_grad_body(ids_ref, keep_ref, got_ref, xc_ref, xs_ref, *refs):
    x_refs, y_refs, full_ref = refs[:4], refs[4:8], refs[8]
    half = full_ref.shape[1] // 2
    full_ref[...] = (mm(keep_ref[...], xc_ref[...], TN) + mm(got_ref[...], xs_ref[...], TN)).astype(BF16)
    rows = full_ref.shape[0] // 16
    for d in range(4):
        bx = lax.rem(ids_ref[2] + d, 4)
        x_refs[d][...] = full_ref[pl.ds(pl.multiple_of(bx * (4 * rows), 4 * rows), 4 * rows), :half]
        by = lax.rem(ids_ref[3] + d, 4)
        for x in range(4):
            y_refs[d][x * rows : (x + 1) * rows] = full_ref[
                pl.ds(pl.multiple_of((4 * x + by) * rows, rows), rows), half:
            ]


def first_sum_body(ids_ref, *refs):
    x_in, y_in, x_out, y_out, total_ref = refs[:4], refs[4:8], refs[8:12], refs[12:16], refs[16]
    rows = x_out[0].shape[0]
    for ins, outs, me in ((x_in, x_out, ids_ref[3]), (y_in, y_out, ids_ref[2])):
        total = ins[0][...].astype(F32)
        for r in ins[1:]:
            total = total + r[...].astype(F32)
        total_ref[...] = total.astype(BF16)
        for d in range(4):
            at = lax.rem(me + d, 4) * rows
            outs[d][...] = total_ref[pl.ds(pl.multiple_of(at, rows), rows)]


def second_sum_body(*refs):
    x_in, y_in, out_ref = refs[:4], refs[4:8], refs[8]
    wide = out_ref.shape[2]
    for ins, base in ((x_in, 0), (y_in, 8)):
        total = ins[0][...].astype(F32)
        for r in ins[1:]:
            total = total + r[...].astype(F32)
        total = total.astype(BF16)
        for n in range(8):
            out_ref[base + n] = total[:, n * wide : (n + 1) * wide]


def unpack_body(slot_ref, back_ref, out_ref):
    tok_rows = out_ref.shape[0]
    slot = jnp.transpose(jnp.broadcast_to(slot_ref[...].astype(F32), (8, tok_rows)))[:, 0:1]
    pick = (iota((tok_rows, SLOTS), 1) == slot.astype(jnp.int32)).astype(BF16)
    out_ref[...] = mm(pick, back_ref[...]).astype(BF16)


def seq_shift(dx, dy):
    return [(4 * x + y, (x + dx) % 4 * 4 + (y + dy) % 4) for x in range(4) for y in range(4)]


def z_shift(d):
    return [(2 * z + c, (z + d) % 8 * 2 + c) for z in range(8) for c in range(2)]


CORES = [(n, n ^ 1) for n in range(16)]


def to_core(data):
    return lax.ppermute(data, "fsdp", CORES)


def spread_slots(data):
    width = data.shape[1]
    out = lax.all_to_all(
        data.reshape(OWNERS, SLOT, width), "seq", split_axis=0, concat_axis=0, tiled=True
    )
    return out.reshape(SLOTS, width)


def gather_weights(block):
    own = [None] * 8
    own[0] = block
    up = down = block
    for step in range(1, 5):
        up = lax.ppermute(up, "fsdp", z_shift(1))
        own[8 - step] = up
        if step < 4:
            down = lax.ppermute(down, "fsdp", z_shift(7))
            own[step] = down
    return own + [to_core(b) for b in own]


def on_device(tokens, assignment, w_query, w_value, out_grad):
    features = tokens[0]
    cotangent = out_grad[0]
    tok_rows, depth = features.shape
    width = w_query.shape[1]
    members = tok_rows
    f = lax.axis_index("fsdp")
    s = lax.axis_index("seq")
    ids = jnp.stack([f // 2, f % 2, s // 4, s % 4]).astype(jnp.int32)
    blocks = gather_weights(jnp.concatenate([w_query, w_value], axis=1))

    px, pg, slot = call(
        pack_body,
        [((SLOTS, depth), BF16), ((SLOTS, width), BF16), ((1, tok_rows), jnp.int32)],
        [vmem()] * 3,
        (assignment, features, cotangent),
        flops=2 * SLOTS * tok_rows * (depth + width),
        moved=2 * (SLOTS + tok_rows) * (depth + width),
    )
    rx = spread_slots(px)
    rg = spread_slots(pg)

    weight_scratch = [pltpu.VMEM((depth, 2 * width), BF16), pltpu.SemaphoreType.DMA((16,))]
    xc, qv, stat, comp, spread, pa = call(
        forward_body,
        [
            ((members, depth), BF16),
            ((members, 2 * width), BF16),
            ((width // HEAD_DIM, 8, members), F32),
            ((members, SLOTS), BF16),
            ((SLOTS, members), BF16),
            ((SLOTS, width), BF16),
        ],
        [smem(), vmem()] + [hbm()] * 16,
        (ids, rx, *blocks),
        scratch=[weight_scratch[0], pltpu.VMEM((members, width), BF16), weight_scratch[1]],
        flops=8 * 10**9,
        moved=16 * 10**6,
    )
    back_a = spread_slots(pa)
    xs = to_core(xc)
    gqv, keep, send = call(
        backward_body,
        [((members, 2 * width), BF16), ((members, width), BF16), ((members, width), BF16)],
        [smem()] + [vmem()] * 4,
        (ids, rg, qv, stat, comp),
        scratch=[
            pltpu.VMEM((members, width), BF16),
            pltpu.VMEM((members, members), BF16),
            pltpu.VMEM((members, members), BF16),
        ],
        flops=6 * 10**9,
        moved=10 * 10**6,
    )
    got = to_core(send)
    (pt,) = call(
        token_grad_body,
        [((SLOTS, depth), BF16)],
        [smem(), vmem(), vmem()] + [hbm()] * 16,
        (ids, gqv, spread, *blocks),
        scratch=weight_scratch,
        flops=4 * 10**9,
        moved=10 * 10**6,
    )
    sums = call(
        weight_grad_body,
        [((width // 4, depth // 2), BF16)] * 8,
        [smem()] + [vmem()] * 4,
        (ids, keep, got, xc, xs),
        scratch=[pltpu.VMEM((width, depth), BF16)],
        flops=3 * 10**9,
        moved=8 * 10**6,
    )
    x_in = [sums[0]] + [lax.ppermute(sums[d], "seq", seq_shift(d, 0)) for d in (1, 2, 3)]
    y_in = [sums[4]] + [lax.ppermute(sums[4 + d], "seq", seq_shift(0, d)) for d in (1, 2, 3)]
    parts = call(
        first_sum_body,
        [((width // 16, depth // 2), BF16)] * 8,
        [smem()] + [vmem()] * 8,
        (ids, *x_in, *y_in),
        scratch=[pltpu.VMEM((width // 4, depth // 2), BF16)],
        moved=3 * 10**6,
    )
    x_in = [parts[0]] + [lax.ppermute(parts[d], "seq", seq_shift(0, d)) for d in (1, 2, 3)]
    y_in = [parts[4]] + [lax.ppermute(parts[4 + d], "seq", seq_shift(d, 0)) for d in (1, 2, 3)]
    (last,) = call(
        second_sum_body,
        [((16, width // 16, depth // 16), BF16)],
        [vmem()] * 8,
        (*x_in, *y_in),
        moved=10**6,
    )
    back_t = spread_slots(pt)
    last = lax.all_to_all(last, "fsdp", split_axis=0, concat_axis=0, tiled=True)
    total = last.astype(F32).reshape(8, 2, width // 16, depth // 16).sum(axis=0)

    def unpack(back, wide):
        return call(
            unpack_body,
            [((tok_rows, wide), BF16)],
            [vmem()] * 2,
            (slot, back),
            flops=2 * SLOTS * tok_rows * wide,
            moved=2 * (SLOTS + tok_rows) * wide,
        )[0]

    attended = unpack(back_a, width)
    token_grad = unpack(back_t, depth)
    return attended[None], token_grad[None], total[0].T, total[1].T


def solution(mesh):
    in_specs = (
        P("fsdp", "seq", None),
        P("fsdp", "seq"),
        P("fsdp", None),
        P("fsdp", None),
        P("fsdp", "seq", None),
    )
    out_specs = (P("fsdp", "seq", None), P("fsdp", "seq", None), P("fsdp", "seq"), P("fsdp", "seq"))
    return jax.shard_map(
        on_device, mesh=mesh, in_specs=in_specs, out_specs=out_specs, check_vma=False
    )
```

```python
import jax
import jax.numpy as jnp
from jax import lax
from jax.experimental import pallas as pl
from jax.experimental.pallas import tpu as pltpu
from jax.sharding import PartitionSpec as P

HEAD_DIM = 128
LOG2E = 1.4426950408889634
BF16 = jnp.bfloat16
F32 = jnp.float32
NN = (((1,), (0,)), ((), ()))
NT = (((1,), (1,)), ((), ()))
TN = (((0,), (0,)), ((), ()))
MIB = 1024 * 1024
SLOT = 48
OWNERS = 16
SLOTS = SLOT * OWNERS


def mm(a, b, dims=NN):
    return lax.dot_general(a, b, dims, preferred_element_type=F32)


def iota(shape, dim):
    return lax.broadcasted_iota(jnp.int32, shape, dim)


def vmem():
    return pl.BlockSpec(memory_space=pltpu.VMEM)


def smem():
    return pl.BlockSpec(memory_space=pltpu.SMEM)


def hbm():
    return pl.BlockSpec(memory_space=pltpu.HBM)


def call(body, outs, ins, args, out_space=vmem, scratch=(), limit=40, flops=0, moved=0):
    return pl.pallas_call(
        body,
        out_shape=[jax.ShapeDtypeStruct(s, d) for s, d in outs],
        in_specs=ins,
        out_specs=[out_space() for _ in outs],
        scratch_shapes=list(scratch),
        compiler_params=pltpu.CompilerParams(vmem_limit_bytes=limit * MIB),
        cost_estimate=pl.CostEstimate(flops=flops, bytes_accessed=moved, transcendentals=0),
    )(*args)


def start(source, target, sem):
    copy = pltpu.make_async_copy(source, target, sem)
    copy.start()
    return copy


def column(row):
    return jnp.transpose(jnp.broadcast_to(row.astype(F32), (8, row.shape[1])))[:, 0:1].astype(jnp.int32)


def pack_body(route_ref, tok_ref, cot_ref, wq_ref, wv_ref, out_ref, slot_ref, w_ref, in_v, out_v, w_v, sems):
    tok_rows, depth = tok_ref.shape
    width = wq_ref.shape[1]
    weight_loads = [
        start(wq_ref, w_v.at[:, :width], sems.at[6]),
        start(wv_ref, w_v.at[:, width:], sems.at[7]),
    ]
    loads = [
        start(tok_ref, in_v.at[:, :depth], sems.at[0]),
        start(cot_ref, in_v.at[:, depth:], sems.at[1]),
    ]
    route = route_ref[...]
    member = iota((OWNERS, tok_rows), 0) == route
    earlier = (iota((tok_rows, tok_rows), 0) < iota((tok_rows, tok_rows), 1)).astype(BF16)
    before = mm(member.astype(BF16), earlier)
    rank = jnp.sum(jnp.where(member, before, 0.0), axis=0, keepdims=True)
    slot = route * SLOT + rank.astype(jnp.int32)
    slot_ref[...] = slot
    for c in weight_loads:
        c.wait()
    stores = [start(w_v, w_ref, sems.at[8])]
    for c in loads:
        c.wait()
    step = 192
    for n in range(SLOTS // step):
        at = n * step
        row = iota((step, tok_rows), 0) + at
        pick = (row == slot).astype(BF16)
        count = jnp.sum((row == route * SLOT + (SLOT - 1)).astype(F32), axis=1, keepdims=True)
        out_v[at : at + step] = (mm(pick, in_v[...]) + count).astype(BF16)
        stores.append(start(out_v.at[at : at + step], out_ref.at[at : at + step], sems.at[2 + n]))
    for c in stores:
        c.wait()


def load_weights(ids_ref, block_refs, w_ref, sems):
    rows = block_refs[0].shape[0]
    z = ids_ref[0]
    c = ids_ref[1]
    copies = []
    for n, block in enumerate(block_refs):
        zb = lax.rem(z + (n % 8), 8)
        fb = 2 * zb + (c if n < 8 else 1 - c)
        copies.append(
            start(block, w_ref.at[pl.ds(pl.multiple_of(fb * rows, rows), rows)], sems.at[n])
        )
    return copies


def masked(scores, lo):
    width = scores.shape[1]
    eye = iota((width, width), 0) == iota((width, width), 1)
    parts = [jnp.where(eye, -1e30, scores[lo : lo + width])]
    if lo:
        parts.insert(0, scores[:lo])
    if lo + width < scores.shape[0]:
        parts.append(scores[lo + width :])
    return jnp.concatenate(parts, axis=0) if len(parts) > 1 else parts[0]


def blocks_of(members):
    return [(lo, min(lo + 128, members)) for lo in range(0, members, 128)]


def positions(rx_ref):
    pick = (iota((OWNERS, SLOTS), 1) == iota((OWNERS, SLOTS), 0) * SLOT + (SLOT - 1)).astype(BF16)
    count = mm(pick, rx_ref[:, 0:128])
    count_t = jnp.transpose(count)[0:8].astype(BF16)
    col = iota((OWNERS, SLOTS), 1)
    first = iota((OWNERS, SLOTS), 0) * SLOT
    past = (col >= first + SLOT).astype(F32)
    inside = ((col >= first) & (col < first + SLOT)).astype(BF16)
    offset = mm(count_t, past.astype(BF16))
    mine = mm(count_t, inside)
    within = iota((8, SLOTS), 1).astype(F32) - SLOT * jnp.sum(past, axis=0, keepdims=True)
    return jnp.where(within < mine, offset + within, -1.0)


def cluster_body(ids_ref, rx_ref, *refs):
    block_refs = refs[:16]
    out_ref, gqv_ref, keep_ref, send_ref = refs[16:20]
    rx_v, w_v, xg_v, xt_v, qv_v, att_v, gqv_v, p_v, d_v, out_v, sems = refs[20:]
    members = xg_v.shape[0]
    depth = xt_v.shape[0]
    width = qv_v.shape[1] // 2
    heads = width // HEAD_DIM
    scaling = HEAD_DIM ** (-0.5)
    factor = scaling * LOG2E
    parts = [slice(0, HEAD_DIM), slice(HEAD_DIM, width)]
    parts += [slice(at, at + width) for at in range(width, depth + width, width)]
    loads = [start(rx_ref.at[:, p], rx_v.at[:, p], sems.at[18 + n]) for n, p in enumerate(parts)]
    weight_copies = load_weights(ids_ref, block_refs, w_v, sems)
    loads[0].wait()
    pos = positions(rx_v)
    comp = (iota((members, SLOTS), 0) == pos[0:1].astype(jnp.int32)).astype(BF16)
    loads[1].wait()
    for at in range(0, depth + width, width):
        if at:
            loads[1 + at // width].wait()
        xg_v[:, at : at + width] = mm(comp, rx_v[:, at : at + width]).astype(BF16)
    xt_v[:, :members] = jnp.transpose(xg_v[:, :depth])
    xt_v[:, members:] = jnp.zeros((depth, xt_v.shape[1] - members), BF16)
    rows = block_refs[0].shape[0]
    shares = []
    for n in range(8):
        to = slice(n * rows, (n + 1) * rows)
        for k, (core, target) in enumerate(((ids_ref[1], keep_ref), (1 - ids_ref[1], send_ref))):
            at = pl.multiple_of((2 * n + core) * rows, rows)
            shares.append(start(xt_v.at[pl.ds(at, rows)], target.at[to], sems.at[24 + 2 * n + k]))
    for c in weight_copies:
        c.wait()
    for at in (0, width):
        qv_v[:, at : at + width] = mm(xg_v[:, :depth], w_v[:, at : at + width]).astype(BF16)

    def head(h):
        at = h * HEAD_DIM
        at_v = width + at
        q = qv_v[:, pl.ds(at, HEAD_DIM)]
        v = qv_v[:, pl.ds(at_v, HEAD_DIM)]
        g = xg_v[:, pl.ds(depth + at, HEAD_DIM)]
        for lo, hi in blocks_of(members):
            scores = masked(mm(q, q[lo:hi], NT), lo)
            top = jnp.max(scores, axis=0, keepdims=True)
            weights = jnp.exp2((scores - top) * factor)
            probs = weights * (1.0 / jnp.sum(weights, axis=0, keepdims=True))
            p_v[:, lo:hi] = probs.astype(BF16)
            grad_probs = mm(v, g[lo:hi], NT)
            row_terms = jnp.sum(probs * grad_probs, axis=0, keepdims=True)
            d_v[:, lo:hi] = (probs * (grad_probs - row_terms) * scaling).astype(BF16)
        probs = p_v[...]
        grad_scores = d_v[...]
        att_v[:, pl.ds(at, HEAD_DIM)] = jnp.transpose(mm(jnp.transpose(v), probs)).astype(BF16)
        gqv_v[:, pl.ds(at_v, HEAD_DIM)] = mm(probs, g).astype(BF16)
        grad_q = mm(grad_scores, q) + jnp.transpose(mm(jnp.transpose(q), grad_scores))
        gqv_v[:, pl.ds(at, HEAD_DIM)] = grad_q.astype(BF16)

    for h in range(heads):
        head(h)
    gqv_copy = start(gqv_v, gqv_ref, sems.at[23])
    spread = (iota((SLOTS, members), 1) == column(pos[0:1])).astype(BF16)
    out_v[:, :width] = mm(spread, att_v[...]).astype(BF16)
    stores = [start(out_v.at[:, :width], out_ref.at[:, :width], sems.at[22])]
    for at in range(0, depth, width):
        grad = mm(gqv_v[...], w_v[at : at + width], NT).astype(BF16)
        to = slice(width + at, 2 * width + at)
        out_v[:, to] = mm(spread, grad).astype(BF16)
        stores.append(start(out_v.at[:, to], out_ref.at[:, to], sems.at[16 + at // width]))
    gqv_copy.wait()
    for c in shares + stores:
        c.wait()


def weight_grad_body(ids_ref, *refs):
    ins, outs, ins_v, full_v, sems = refs[:4], refs[4:7], refs[7:11], refs[11], refs[12]
    copies = [start(r, v, sems.at[n]) for n, (r, v) in enumerate(zip(ins, ins_v))]
    keep_v, own_v, xs_v, got_v = ins_v
    keep_ref, a_ref, b_ref = outs
    width = a_ref.shape[1]
    rows = a_ref.shape[0] // 4
    members = own_v.shape[0]
    parity = lax.rem(ids_ref[0], 2)
    for c in copies:
        c.wait()
    stores = []
    for half in (0, 1):
        cols = slice(half * width, (half + 1) * width)
        full_v[:, cols] = (mm(keep_v[:, :members], own_v[:, cols]) + mm(xs_v[:, :members], got_v[:, cols])).astype(BF16)
        for n in range(4):
            to = slice(n * rows, (n + 1) * rows)
            mine = pl.multiple_of((2 * n + parity) * rows, rows)
            other = pl.multiple_of((2 * n + 1 - parity) * rows, rows)
            at = 4 + 8 * half + 2 * n
            stores.append(
                start(full_v.at[pl.ds(mine, rows), cols], keep_ref.at[to, cols], sems.at[at])
            )
            stores.append(
                start(full_v.at[pl.ds(other, rows), cols], (a_ref, b_ref)[half].at[to], sems.at[at + 1])
            )
    for c in stores:
        c.wait()


def pair_sum_body(ids_ref, keep_ref, a_ref, b_ref, *refs):
    outs, total_ref = refs[:3], refs[3]
    width = a_ref.shape[1]
    rows = outs[0].shape[0] // 2
    total_ref[:, :width] = (keep_ref[:, :width].astype(F32) + a_ref[...].astype(F32)).astype(BF16)
    total_ref[:, width:] = (keep_ref[:, width:].astype(F32) + b_ref[...].astype(F32)).astype(BF16)
    bit = lax.rem(lax.div(ids_ref[0], 2), 2)
    for n in range(2):
        to = slice(n * rows, (n + 1) * rows)
        mine = pl.ds(pl.multiple_of((2 * n + bit) * rows, rows), rows)
        other = pl.ds(pl.multiple_of((2 * n + 1 - bit) * rows, rows), rows)
        outs[0][to] = total_ref[mine]
        outs[1][to] = total_ref[other, :width]
        outs[2][to] = total_ref[other, width:]


def quad_sum_body(keep_ref, a_ref, b_ref, out_ref):
    width = a_ref.shape[1]
    tall = out_ref.shape[1]
    low = tall // 3
    cols = width // OWNERS
    spare = out_ref.shape[2] - 2 * cols
    q = (keep_ref[:, :width].astype(F32) + a_ref[...].astype(F32)).astype(BF16)
    v = (keep_ref[:, width:].astype(F32) + b_ref[...].astype(F32)).astype(BF16)
    for n in range(OWNERS):
        qn = q[:, n * cols : (n + 1) * cols]
        vn = v[:, n * cols : (n + 1) * cols]
        out_ref[n, :, :cols] = qn[:tall]
        out_ref[n, :, cols : 2 * cols] = vn[:tall]
        rest = jnp.concatenate([qn[tall:], vn[tall:]], axis=1)
        for k in range(3):
            out_ref[n, k * low : (k + 1) * low, 2 * cols :] = rest[:, k * spare : (k + 1) * spare]


def seq_sum_body(ids_ref, in_ref, keep_ref, send_ref):
    total = in_ref[0].astype(F32)
    for n in range(1, OWNERS):
        total = total + in_ref[n].astype(F32)
    rows, cols = keep_ref.shape
    tall = total.shape[0]
    rest = total[:, cols:]
    third = tall // 3
    rest = jnp.concatenate([rest[k * third : (k + 1) * third] for k in range(3)], axis=1)
    total = jnp.concatenate([total[:, :cols], rest], axis=0)
    low = ids_ref[0] < 4
    keep_ref[...] = jnp.where(low, total[:rows], total[rows:])
    send_ref[...] = jnp.where(low, total[rows:], total[:rows])


def last_sum_body(keep_ref, got_ref, q_ref, v_ref):
    total = jnp.transpose(keep_ref[...] + got_ref[...])
    cols = q_ref.shape[0]
    q_ref[...] = total[:cols]
    v_ref[...] = total[cols:]


def unpack_body(slot_ref, back_ref, att_ref, grad_ref, back_v, out_v, sems):
    tok_rows, width = att_ref.shape
    parts = [slice(at, at + width) for at in range(0, back_v.shape[1], width)]
    loads = [start(back_ref.at[:, p], back_v.at[:, p], sems.at[n]) for n, p in enumerate(parts)]
    pick = (iota((tok_rows, SLOTS), 1) == column(slot_ref[...])).astype(BF16)
    stores = []
    for n, p in enumerate(parts):
        loads[n].wait()
        out_v[:, p] = mm(pick, back_v[:, p]).astype(BF16)
        target = grad_ref.at[:, p.start - width : p.stop - width] if n else att_ref
        stores.append(start(out_v.at[:, p], target, sems.at[len(parts) + n]))
    for c in stores:
        c.wait()


def z_shift(d):
    return [(2 * z + c, (z + d) % 8 * 2 + c) for z in range(8) for c in range(2)]


def z_pair(odd):
    return [
        (2 * z + c, ((z ^ 1) if not odd else (z + 1 if z % 2 else z - 1) % 8) * 2 + c)
        for z in range(8)
        for c in range(2)
    ]


def z_two(odd):
    return [
        (2 * z + c, (z + (2 if (z % 4 < 2) != bool(odd) else -2)) % 8 * 2 + c)
        for z in range(8)
        for c in range(2)
    ]


CORES = [(n, n ^ 1) for n in range(16)]


def to_core(data):
    return lax.ppermute(data, "fsdp", CORES)


def spread_slots(data):
    width = data.shape[1]
    out = lax.all_to_all(
        data.reshape(OWNERS, SLOT, width), "seq", split_axis=0, concat_axis=0, tiled=True
    )
    return out.reshape(SLOTS, width)


def gather_weights(block):
    own = [None] * 8
    own[0] = block
    up = down = block
    for step in range(1, 5):
        up = lax.ppermute(up, "fsdp", z_shift(1))
        own[8 - step] = up
        if step < 4:
            down = lax.ppermute(down, "fsdp", z_shift(7))
            own[step] = down
    return own + [to_core(b) for b in own]


def on_device(tokens, assignment, w_query, w_value, out_grad):
    features = tokens[0]
    cotangent = out_grad[0]
    tok_rows, depth = features.shape
    width = w_query.shape[1]
    members = tok_rows
    f = lax.axis_index("fsdp")
    ids = jnp.stack([f // 2, f % 2]).astype(jnp.int32)
    both = depth + width
    padded = -(-members // 128) * 128
    sems = pltpu.SemaphoreType.DMA
    packed, slot, block = pl.pallas_call(
        pack_body,
        out_shape=[
            jax.ShapeDtypeStruct((SLOTS, both), BF16),
            jax.ShapeDtypeStruct((1, tok_rows), jnp.int32),
            jax.ShapeDtypeStruct((depth // 16, 2 * width), BF16),
        ],
        in_specs=[vmem(), hbm(), hbm(), hbm(), hbm()],
        out_specs=[hbm(), vmem(), hbm()],
        scratch_shapes=[
            pltpu.VMEM((tok_rows, both), BF16),
            pltpu.VMEM((SLOTS, both), BF16),
            pltpu.VMEM((depth // 16, 2 * width), BF16),
            sems((9,)),
        ],
        compiler_params=pltpu.CompilerParams(vmem_limit_bytes=60 * MIB),
        cost_estimate=pl.CostEstimate(
            flops=2 * SLOTS * tok_rows * both, bytes_accessed=2 * (SLOTS + tok_rows) * both, transcendentals=0
        ),
    )(assignment, features, cotangent, w_query, w_value)
    blocks = gather_weights(block)
    received = spread_slots(packed)
    result, gqv, keep, send = call(
        cluster_body,
        [
            ((SLOTS, both), BF16),
            ((members, 2 * width), BF16),
            ((depth // 2, padded), BF16),
            ((depth // 2, padded), BF16),
        ],
        [smem()] + [hbm()] * 17,
        (ids, received, *blocks),
        out_space=hbm,
        scratch=[
            pltpu.VMEM((SLOTS, both), BF16),
            pltpu.VMEM((depth, 2 * width), BF16),
            pltpu.VMEM((members, both), BF16),
            pltpu.VMEM((depth, padded), BF16),
            pltpu.VMEM((members, 2 * width), BF16),
            pltpu.VMEM((members, width), BF16),
            pltpu.VMEM((members, 2 * width), BF16),
            pltpu.VMEM((members, members), BF16),
            pltpu.VMEM((members, members), BF16),
            pltpu.VMEM((SLOTS, both), BF16),
            sems((40,)),
        ],
        limit=48,
        flops=16 * 10**9,
        moved=20 * 10**6,
    )
    xs = to_core(send)
    got = to_core(gqv)
    back = spread_slots(result)
    rows = depth // 16
    keep, part_a, part_b = call(
        weight_grad_body,
        [((4 * rows, 2 * width), BF16), ((4 * rows, width), BF16), ((4 * rows, width), BF16)],
        [smem()] + [hbm()] * 4,
        (ids, keep, gqv, xs, got),
        out_space=hbm,
        scratch=[
            pltpu.VMEM((depth // 2, padded), BF16),
            pltpu.VMEM((members, 2 * width), BF16),
            pltpu.VMEM((depth // 2, padded), BF16),
            pltpu.VMEM((members, 2 * width), BF16),
            pltpu.VMEM((depth // 2, 2 * width), BF16),
            sems((20,)),
        ],
        limit=40,
        flops=3 * 10**9,
        moved=8 * 10**6,
    )
    part_a = lax.ppermute(part_a, "fsdp", z_pair(0))
    part_b = lax.ppermute(part_b, "fsdp", z_pair(1))
    keep, part_a, part_b = call(
        pair_sum_body,
        [((2 * rows, 2 * width), BF16), ((2 * rows, width), BF16), ((2 * rows, width), BF16)],
        [smem()] + [vmem()] * 3,
        (ids, keep, part_a, part_b),
        scratch=[pltpu.VMEM((4 * rows, 2 * width), BF16)],
        moved=4 * 10**6,
    )
    part_a = lax.ppermute(part_a, "fsdp", z_two(0))
    part_b = lax.ppermute(part_b, "fsdp", z_two(1))
    (last,) = call(
        quad_sum_body,
        [((OWNERS, rows * width // 512, 128), BF16)],
        [vmem()] * 3,
        (keep, part_a, part_b),
        moved=2 * 10**6,
    )
    last, back = lax.optimization_barrier((last, back))
    last = lax.all_to_all(last, "seq", split_axis=0, concat_axis=0, tiled=True)
    attended, token_grad = call(
        unpack_body,
        [((tok_rows, width), BF16), ((tok_rows, depth), BF16)],
        [vmem(), hbm()],
        (slot, back),
        out_space=hbm,
        scratch=[pltpu.VMEM((SLOTS, both), BF16), pltpu.VMEM((tok_rows, both), BF16), sems((6,))],
        limit=60,
        flops=2 * SLOTS * tok_rows * both,
        moved=2 * (SLOTS + tok_rows) * both,
    )
    last, attended, token_grad = lax.optimization_barrier((last, attended, token_grad))
    keep, send = call(
        seq_sum_body,
        [((rows, width // 8), F32)] * 2,
        [smem(), vmem()],
        (ids, last),
        moved=10**6,
    )
    got = lax.ppermute(send, "fsdp", z_shift(4))
    grad_wq, grad_wv = call(
        last_sum_body, [((width // 16, rows), F32)] * 2, [vmem()] * 2, (keep, got), moved=10**5
    )
    return attended[None], token_grad[None], grad_wq.T, grad_wv.T


def solution(mesh):
    in_specs = (
        P("fsdp", "seq", None),
        P("fsdp", "seq"),
        P("fsdp", None),
        P("fsdp", None),
        P("fsdp", "seq", None),
    )
    out_specs = (P("fsdp", "seq", None), P("fsdp", "seq", None), P("fsdp", "seq"), P("fsdp", "seq"))
    return jax.shard_map(
        on_device, mesh=mesh, in_specs=in_specs, out_specs=out_specs, check_vma=False
    )
```

```python
import jax
import jax.numpy as jnp
from jax import lax
from jax.experimental import pallas as pl
from jax.experimental.pallas import tpu as pltpu
from jax.sharding import PartitionSpec as P

HEAD_DIM = 128
LOG2E = 1.4426950408889634
BF16 = jnp.bfloat16
F32 = jnp.float32
NN = (((1,), (0,)), ((), ()))
NT = (((1,), (1,)), ((), ()))
TN = (((0,), (0,)), ((), ()))
MIB = 1024 * 1024
SLOT = 48
OWNERS = 16
SLOTS = SLOT * OWNERS


def mm(a, b, dims=NN):
    return lax.dot_general(a, b, dims, preferred_element_type=F32)


def iota(shape, dim):
    return lax.broadcasted_iota(jnp.int32, shape, dim)


def vmem():
    return pl.BlockSpec(memory_space=pltpu.VMEM)


def smem():
    return pl.BlockSpec(memory_space=pltpu.SMEM)


def hbm():
    return pl.BlockSpec(memory_space=pltpu.HBM)


def call(body, outs, ins, args, out_space=vmem, scratch=(), limit=40, flops=0, moved=0):
    return pl.pallas_call(
        body,
        out_shape=[jax.ShapeDtypeStruct(s, d) for s, d in outs],
        in_specs=ins,
        out_specs=[out_space() for _ in outs],
        scratch_shapes=list(scratch),
        compiler_params=pltpu.CompilerParams(vmem_limit_bytes=limit * MIB),
        cost_estimate=pl.CostEstimate(flops=flops, bytes_accessed=moved, transcendentals=0),
    )(*args)


def start(source, target, sem):
    copy = pltpu.make_async_copy(source, target, sem)
    copy.start()
    return copy


def column(row):
    return jnp.transpose(jnp.broadcast_to(row.astype(F32), (8, row.shape[1])))[:, 0:1].astype(jnp.int32)


def pack_body(route_ref, tok_ref, cot_ref, wq_ref, wv_ref, out_ref, slot_ref, w_ref, in_v, out_v, w_v, route_v, slot_v, sems):
    tok_rows, depth = tok_ref.shape
    route_load = start(route_ref, route_v, sems.at[9])
    width = wq_ref.shape[1]
    weight_loads = [
        start(wq_ref, w_v.at[:, :width], sems.at[6]),
        start(wv_ref, w_v.at[:, width:], sems.at[7]),
    ]
    loads = [
        start(tok_ref, in_v.at[:, :depth], sems.at[0]),
        start(cot_ref, in_v.at[:, depth:], sems.at[1]),
    ]
    route_load.wait()
    route = route_v[...]
    member = iota((OWNERS, tok_rows), 0) == route
    earlier = (iota((tok_rows, tok_rows), 0) < iota((tok_rows, tok_rows), 1)).astype(BF16)
    before = mm(member.astype(BF16), earlier)
    rank = jnp.sum(jnp.where(member, before, 0.0), axis=0, keepdims=True)
    slot = route * SLOT + rank.astype(jnp.int32)
    slot_v[...] = slot
    for c in weight_loads:
        c.wait()
    stores = [start(w_v, w_ref, sems.at[8]), start(slot_v, slot_ref, sems.at[10])]
    for c in loads:
        c.wait()
    step = 192
    for n in range(SLOTS // step):
        at = n * step
        row = iota((step, tok_rows), 0) + at
        pick = (row == slot).astype(BF16)
        count = jnp.sum((row == route * SLOT + (SLOT - 1)).astype(F32), axis=1, keepdims=True)
        out_v[at : at + step] = (mm(pick, in_v[...]) + count).astype(BF16)
        stores.append(start(out_v.at[at : at + step], out_ref.at[at : at + step], sems.at[2 + n]))
    for c in stores:
        c.wait()


def load_weights(ids_ref, block_refs, w_ref, sems):
    rows = block_refs[0].shape[0]
    z = ids_ref[0]
    c = ids_ref[1]
    copies = []
    for n, block in enumerate(block_refs):
        zb = lax.rem(z + (n % 8), 8)
        fb = 2 * zb + (c if n < 8 else 1 - c)
        copies.append(
            start(block, w_ref.at[pl.ds(pl.multiple_of(fb * rows, rows), rows)], sems.at[n])
        )
    return copies


def masked(scores, lo):
    width = scores.shape[1]
    eye = iota((width, width), 0) == iota((width, width), 1)
    parts = [jnp.where(eye, -1e30, scores[lo : lo + width])]
    if lo:
        parts.insert(0, scores[:lo])
    if lo + width < scores.shape[0]:
        parts.append(scores[lo + width :])
    return jnp.concatenate(parts, axis=0) if len(parts) > 1 else parts[0]


def blocks_of(members):
    return [(lo, min(lo + 128, members)) for lo in range(0, members, 128)]


def positions(rx_ref):
    pick = (iota((OWNERS, SLOTS), 1) == iota((OWNERS, SLOTS), 0) * SLOT + (SLOT - 1)).astype(BF16)
    count = mm(pick, rx_ref[:, 0:128])
    count_t = jnp.transpose(count)[0:8].astype(BF16)
    col = iota((OWNERS, SLOTS), 1)
    first = iota((OWNERS, SLOTS), 0) * SLOT
    past = (col >= first + SLOT).astype(F32)
    inside = ((col >= first) & (col < first + SLOT)).astype(BF16)
    offset = mm(count_t, past.astype(BF16))
    mine = mm(count_t, inside)
    within = iota((8, SLOTS), 1).astype(F32) - SLOT * jnp.sum(past, axis=0, keepdims=True)
    return jnp.where(within < mine, offset + within, -1.0)


def cluster_body(ids_hbm, rx_ref, *refs):
    block_refs = refs[:16]
    out_ref, gqv_ref, keep_ref, send_ref = refs[16:20]
    rx_v, w_v, xg_v, xt_v, qv_v, att_v, gqv_v, p_v, d_v, out_v, ids_ref, sems = refs[20:]
    members = xg_v.shape[0]
    depth = xt_v.shape[0]
    width = qv_v.shape[1] // 2
    heads = width // HEAD_DIM
    scaling = HEAD_DIM ** (-0.5)
    factor = scaling * LOG2E
    parts = [slice(0, HEAD_DIM), slice(HEAD_DIM, width)]
    parts += [slice(at, at + width) for at in range(width, depth + width, width)]
    loads = [start(rx_ref.at[:, p], rx_v.at[:, p], sems.at[18 + n]) for n, p in enumerate(parts)]
    start(ids_hbm, ids_ref, sems.at[40]).wait()
    weight_copies = load_weights(ids_ref, block_refs, w_v, sems)
    loads[0].wait()
    pos = positions(rx_v)
    comp = (iota((members, SLOTS), 0) == pos[0:1].astype(jnp.int32)).astype(BF16)
    loads[1].wait()
    for at in range(0, depth + width, width):
        if at:
            loads[1 + at // width].wait()
        xg_v[:, at : at + width] = mm(comp, rx_v[:, at : at + width]).astype(BF16)
    xt_v[:, :members] = jnp.transpose(xg_v[:, :depth])
    xt_v[:, members:] = jnp.zeros((depth, xt_v.shape[1] - members), BF16)
    rows = block_refs[0].shape[0]
    shares = []
    for n in range(8):
        to = slice(n * rows, (n + 1) * rows)
        for k, (core, target) in enumerate(((ids_ref[1], keep_ref), (1 - ids_ref[1], send_ref))):
            at = pl.multiple_of((2 * n + core) * rows, rows)
            shares.append(start(xt_v.at[pl.ds(at, rows)], target.at[to], sems.at[24 + 2 * n + k]))
    for c in weight_copies:
        c.wait()
    for at in (0, width):
        qv_v[:, at : at + width] = mm(xg_v[:, :depth], w_v[:, at : at + width]).astype(BF16)

    def head(h):
        at = h * HEAD_DIM
        at_v = width + at
        q = qv_v[:, pl.ds(at, HEAD_DIM)]
        v = qv_v[:, pl.ds(at_v, HEAD_DIM)]
        g = xg_v[:, pl.ds(depth + at, HEAD_DIM)]
        for lo, hi in blocks_of(members):
            scores = masked(mm(q, q[lo:hi], NT), lo)
            top = jnp.max(scores, axis=0, keepdims=True)
            weights = jnp.exp2((scores - top) * factor)
            probs = weights * (1.0 / jnp.sum(weights, axis=0, keepdims=True))
            p_v[:, lo:hi] = probs.astype(BF16)
            grad_probs = mm(v, g[lo:hi], NT)
            row_terms = jnp.sum(probs * grad_probs, axis=0, keepdims=True)
            d_v[:, lo:hi] = (probs * (grad_probs - row_terms) * scaling).astype(BF16)
        probs = p_v[...]
        grad_scores = d_v[...]
        att_v[:, pl.ds(at, HEAD_DIM)] = jnp.transpose(mm(jnp.transpose(v), probs)).astype(BF16)
        gqv_v[:, pl.ds(at_v, HEAD_DIM)] = mm(probs, g).astype(BF16)
        grad_q = mm(grad_scores, q) + jnp.transpose(mm(jnp.transpose(q), grad_scores))
        gqv_v[:, pl.ds(at, HEAD_DIM)] = grad_q.astype(BF16)

    for h in range(heads):
        head(h)
    gqv_copy = start(gqv_v, gqv_ref, sems.at[23])
    spread = (iota((SLOTS, members), 1) == column(pos[0:1])).astype(BF16)
    out_v[:, :width] = mm(spread, att_v[...]).astype(BF16)
    stores = [start(out_v.at[:, :width], out_ref.at[:, :width], sems.at[22])]
    for at in range(0, depth, width):
        grad = mm(gqv_v[...], w_v[at : at + width], NT).astype(BF16)
        to = slice(width + at, 2 * width + at)
        out_v[:, to] = mm(spread, grad).astype(BF16)
        stores.append(start(out_v.at[:, to], out_ref.at[:, to], sems.at[16 + at // width]))
    gqv_copy.wait()
    for c in shares + stores:
        c.wait()


def weight_grad_body(ids_hbm, *refs):
    ins, outs, ins_v, full_v, ids_ref, sems = refs[:4], refs[4:7], refs[7:11], refs[11], refs[12], refs[13]
    copies = [start(r, v, sems.at[n]) for n, (r, v) in enumerate(zip(ins, ins_v))]
    copies.append(start(ids_hbm, ids_ref, sems.at[20]))
    keep_v, own_v, xs_v, got_v = ins_v
    keep_ref, a_ref, b_ref = outs
    width = a_ref.shape[1]
    rows = a_ref.shape[0] // 4
    members = own_v.shape[0]
    for c in copies:
        c.wait()
    parity = lax.rem(ids_ref[0], 2)
    stores = []
    for half in (0, 1):
        cols = slice(half * width, (half + 1) * width)
        full_v[:, cols] = (mm(keep_v[:, :members], own_v[:, cols]) + mm(xs_v[:, :members], got_v[:, cols])).astype(BF16)
        for n in range(4):
            to = slice(n * rows, (n + 1) * rows)
            mine = pl.multiple_of((2 * n + parity) * rows, rows)
            other = pl.multiple_of((2 * n + 1 - parity) * rows, rows)
            at = 4 + 8 * half + 2 * n
            stores.append(
                start(full_v.at[pl.ds(mine, rows), cols], keep_ref.at[to, cols], sems.at[at])
            )
            stores.append(
                start(full_v.at[pl.ds(other, rows), cols], (a_ref, b_ref)[half].at[to], sems.at[at + 1])
            )
    for c in stores:
        c.wait()


def pair_sum_body(ids_ref, keep_ref, a_ref, b_ref, *refs):
    outs, total_ref = refs[:3], refs[3]
    width = a_ref.shape[1]
    rows = outs[0].shape[0] // 2
    total_ref[:, :width] = (keep_ref[:, :width].astype(F32) + a_ref[...].astype(F32)).astype(BF16)
    total_ref[:, width:] = (keep_ref[:, width:].astype(F32) + b_ref[...].astype(F32)).astype(BF16)
    bit = lax.rem(lax.div(ids_ref[0], 2), 2)
    for n in range(2):
        to = slice(n * rows, (n + 1) * rows)
        mine = pl.ds(pl.multiple_of((2 * n + bit) * rows, rows), rows)
        other = pl.ds(pl.multiple_of((2 * n + 1 - bit) * rows, rows), rows)
        outs[0][to] = total_ref[mine]
        outs[1][to] = total_ref[other, :width]
        outs[2][to] = total_ref[other, width:]


def quad_sum_body(keep_ref, a_ref, b_ref, out_ref):
    width = a_ref.shape[1]
    tall = out_ref.shape[1]
    low = tall // 3
    cols = width // OWNERS
    spare = out_ref.shape[2] - 2 * cols
    q = (keep_ref[:, :width].astype(F32) + a_ref[...].astype(F32)).astype(BF16)
    v = (keep_ref[:, width:].astype(F32) + b_ref[...].astype(F32)).astype(BF16)
    for n in range(OWNERS):
        qn = q[:, n * cols : (n + 1) * cols]
        vn = v[:, n * cols : (n + 1) * cols]
        out_ref[n, :, :cols] = qn[:tall]
        out_ref[n, :, cols : 2 * cols] = vn[:tall]
        rest = jnp.concatenate([qn[tall:], vn[tall:]], axis=1)
        for k in range(3):
            out_ref[n, k * low : (k + 1) * low, 2 * cols :] = rest[:, k * spare : (k + 1) * spare]


def seq_sum_body(ids_ref, in_ref, keep_ref, send_ref):
    total = in_ref[0].astype(F32)
    for n in range(1, OWNERS):
        total = total + in_ref[n].astype(F32)
    rows, cols = keep_ref.shape
    tall = total.shape[0]
    rest = total[:, cols:]
    third = tall // 3
    rest = jnp.concatenate([rest[k * third : (k + 1) * third] for k in range(3)], axis=1)
    total = jnp.concatenate([total[:, :cols], rest], axis=0)
    low = ids_ref[0] < 4
    keep_ref[...] = jnp.where(low, total[:rows], total[rows:])
    send_ref[...] = jnp.where(low, total[rows:], total[:rows])


def last_sum_body(keep_ref, got_ref, q_ref, v_ref):
    total = jnp.transpose(keep_ref[...] + got_ref[...])
    cols = q_ref.shape[0]
    q_ref[...] = total[:cols]
    v_ref[...] = total[cols:]


def unpack_body(slot_ref, back_ref, att_ref, grad_ref, back_v, out_v, sems):
    tok_rows, width = att_ref.shape
    parts = [slice(at, at + width) for at in range(0, back_v.shape[1], width)]
    loads = [start(back_ref.at[:, p], back_v.at[:, p], sems.at[n]) for n, p in enumerate(parts)]
    pick = (iota((tok_rows, SLOTS), 1) == column(slot_ref[...])).astype(BF16)
    stores = []
    for n, p in enumerate(parts):
        loads[n].wait()
        out_v[:, p] = mm(pick, back_v[:, p]).astype(BF16)
        target = grad_ref.at[:, p.start - width : p.stop - width] if n else att_ref
        stores.append(start(out_v.at[:, p], target, sems.at[len(parts) + n]))
    for c in stores:
        c.wait()


def z_shift(d):
    return [(2 * z + c, (z + d) % 8 * 2 + c) for z in range(8) for c in range(2)]


def z_pair(odd):
    return [
        (2 * z + c, ((z ^ 1) if not odd else (z + 1 if z % 2 else z - 1) % 8) * 2 + c)
        for z in range(8)
        for c in range(2)
    ]


def z_two(odd):
    return [
        (2 * z + c, (z + (2 if (z % 4 < 2) != bool(odd) else -2)) % 8 * 2 + c)
        for z in range(8)
        for c in range(2)
    ]


CORES = [(n, n ^ 1) for n in range(16)]


def to_core(data):
    return lax.ppermute(data, "fsdp", CORES)


def spread_slots(data):
    width = data.shape[1]
    out = lax.all_to_all(
        data.reshape(OWNERS, SLOT, width), "seq", split_axis=0, concat_axis=0, tiled=True
    )
    return out.reshape(SLOTS, width)


def gather_weights(block):
    own = [None] * 8
    own[0] = block
    up = down = block
    for step in range(1, 5):
        up = lax.ppermute(up, "fsdp", z_shift(1))
        own[8 - step] = up
        if step < 4:
            down = lax.ppermute(down, "fsdp", z_shift(7))
            own[step] = down
    return own + [to_core(b) for b in own]


def on_device(tokens, assignment, w_query, w_value, out_grad):
    features = tokens[0]
    cotangent = out_grad[0]
    tok_rows, depth = features.shape
    width = w_query.shape[1]
    members = tok_rows
    f = lax.axis_index("fsdp")
    ids = jnp.stack([f // 2, f % 2]).astype(jnp.int32)
    both = depth + width
    padded = -(-members // 128) * 128
    sems = pltpu.SemaphoreType.DMA
    packed, slot, block = pl.pallas_call(
        pack_body,
        out_shape=[
            jax.ShapeDtypeStruct((SLOTS, both), BF16),
            jax.ShapeDtypeStruct((1, tok_rows), jnp.int32),
            jax.ShapeDtypeStruct((depth // 16, 2 * width), BF16),
        ],
        in_specs=[hbm()] * 5,
        out_specs=[hbm()] * 3,
        scratch_shapes=[
            pltpu.VMEM((tok_rows, both), BF16),
            pltpu.VMEM((SLOTS, both), BF16),
            pltpu.VMEM((depth // 16, 2 * width), BF16),
            pltpu.VMEM((1, tok_rows), jnp.int32),
            pltpu.VMEM((1, tok_rows), jnp.int32),
            sems((11,)),
        ],
        compiler_params=pltpu.CompilerParams(vmem_limit_bytes=60 * MIB),
        cost_estimate=pl.CostEstimate(
            flops=2 * SLOTS * tok_rows * both, bytes_accessed=2 * (SLOTS + tok_rows) * both, transcendentals=0
        ),
    )(assignment, features, cotangent, w_query, w_value)
    blocks = gather_weights(block)
    received = spread_slots(packed)
    result, gqv, keep, send = call(
        cluster_body,
        [
            ((SLOTS, both), BF16),
            ((members, 2 * width), BF16),
            ((depth // 2, padded), BF16),
            ((depth // 2, padded), BF16),
        ],
        [hbm()] * 18,
        (ids, received, *blocks),
        out_space=hbm,
        scratch=[
            pltpu.VMEM((SLOTS, both), BF16),
            pltpu.VMEM((depth, 2 * width), BF16),
            pltpu.VMEM((members, both), BF16),
            pltpu.VMEM((depth, padded), BF16),
            pltpu.VMEM((members, 2 * width), BF16),
            pltpu.VMEM((members, width), BF16),
            pltpu.VMEM((members, 2 * width), BF16),
            pltpu.VMEM((members, members), BF16),
            pltpu.VMEM((members, members), BF16),
            pltpu.VMEM((SLOTS, both), BF16),
            pltpu.SMEM((2,), jnp.int32),
            sems((41,)),
        ],
        limit=50,
        flops=16 * 10**9,
        moved=20 * 10**6,
    )
    xs = to_core(send)
    got = to_core(gqv)
    back = spread_slots(result)
    rows = depth // 16
    keep, part_a, part_b = call(
        weight_grad_body,
        [((4 * rows, 2 * width), BF16), ((4 * rows, width), BF16), ((4 * rows, width), BF16)],
        [hbm()] * 5,
        (ids, keep, gqv, xs, got),
        out_space=hbm,
        scratch=[
            pltpu.VMEM((depth // 2, padded), BF16),
            pltpu.VMEM((members, 2 * width), BF16),
            pltpu.VMEM((depth // 2, padded), BF16),
            pltpu.VMEM((members, 2 * width), BF16),
            pltpu.VMEM((depth // 2, 2 * width), BF16),
            pltpu.SMEM((2,), jnp.int32),
            sems((21,)),
        ],
        limit=40,
        flops=3 * 10**9,
        moved=8 * 10**6,
    )
    part_a = lax.ppermute(part_a, "fsdp", z_pair(0))
    part_b = lax.ppermute(part_b, "fsdp", z_pair(1))
    keep, part_a, part_b = call(
        pair_sum_body,
        [((2 * rows, 2 * width), BF16), ((2 * rows, width), BF16), ((2 * rows, width), BF16)],
        [smem()] + [vmem()] * 3,
        (ids, keep, part_a, part_b),
        scratch=[pltpu.VMEM((4 * rows, 2 * width), BF16)],
        moved=4 * 10**6,
    )
    part_a = lax.ppermute(part_a, "fsdp", z_two(0))
    part_b = lax.ppermute(part_b, "fsdp", z_two(1))
    (last,) = call(
        quad_sum_body,
        [((OWNERS, rows * width // 512, 128), BF16)],
        [vmem()] * 3,
        (keep, part_a, part_b),
        moved=2 * 10**6,
    )
    last, back = lax.optimization_barrier((last, back))
    last = lax.all_to_all(last, "seq", split_axis=0, concat_axis=0, tiled=True)
    attended, token_grad = call(
        unpack_body,
        [((tok_rows, width), BF16), ((tok_rows, depth), BF16)],
        [vmem(), hbm()],
        (slot, back),
        out_space=hbm,
        scratch=[pltpu.VMEM((SLOTS, both), BF16), pltpu.VMEM((tok_rows, both), BF16), sems((6,))],
        limit=60,
        flops=2 * SLOTS * tok_rows * both,
        moved=2 * (SLOTS + tok_rows) * both,
    )
    last, attended, token_grad = lax.optimization_barrier((last, attended, token_grad))
    keep, send = call(
        seq_sum_body,
        [((rows, width // 8), F32)] * 2,
        [smem(), vmem()],
        (ids, last),
        moved=10**6,
    )
    got = lax.ppermute(send, "fsdp", z_shift(4))
    grad_wq, grad_wv = call(
        last_sum_body, [((width // 16, rows), F32)] * 2, [vmem()] * 2, (keep, got), moved=10**5
    )
    return attended[None], token_grad[None], grad_wq.T, grad_wv.T


def solution(mesh):
    in_specs = (
        P("fsdp", "seq", None),
        P("fsdp", "seq"),
        P("fsdp", None),
        P("fsdp", None),
        P("fsdp", "seq", None),
    )
    out_specs = (P("fsdp", "seq", None), P("fsdp", "seq", None), P("fsdp", "seq"), P("fsdp", "seq"))
    return jax.shard_map(
        on_device, mesh=mesh, in_specs=in_specs, out_specs=out_specs, check_vma=False
    )
```

```python
import jax
import jax.numpy as jnp
from jax import lax
from jax.experimental import pallas as pl
from jax.experimental.pallas import tpu as pltpu
from jax.sharding import PartitionSpec as P

HEAD_DIM = 128
LOG2E = 1.4426950408889634
BF16 = jnp.bfloat16
F32 = jnp.float32
NN = (((1,), (0,)), ((), ()))
NT = (((1,), (1,)), ((), ()))
TN = (((0,), (0,)), ((), ()))
MIB = 1024 * 1024
SLOT = 48
OWNERS = 16
SLOTS = SLOT * OWNERS


def mm(a, b, dims=NN):
    return lax.dot_general(a, b, dims, preferred_element_type=F32)


def iota(shape, dim):
    return lax.broadcasted_iota(jnp.int32, shape, dim)


def vmem():
    return pl.BlockSpec(memory_space=pltpu.VMEM)


def smem():
    return pl.BlockSpec(memory_space=pltpu.SMEM)


def hbm():
    return pl.BlockSpec(memory_space=pltpu.HBM)


def call(body, outs, ins, args, out_space=vmem, scratch=(), limit=40, flops=0, moved=0):
    return pl.pallas_call(
        body,
        out_shape=[jax.ShapeDtypeStruct(s, d) for s, d in outs],
        in_specs=ins,
        out_specs=[out_space() for _ in outs],
        scratch_shapes=list(scratch),
        compiler_params=pltpu.CompilerParams(vmem_limit_bytes=limit * MIB),
        cost_estimate=pl.CostEstimate(flops=flops, bytes_accessed=moved, transcendentals=0),
    )(*args)


def start(source, target, sem):
    copy = pltpu.make_async_copy(source, target, sem)
    copy.start()
    return copy


def column(row):
    return jnp.transpose(jnp.broadcast_to(row.astype(F32), (8, row.shape[1])))[:, 0:1].astype(jnp.int32)


def pack_body(route_ref, tok_ref, cot_ref, wq_ref, wv_ref, out_ref, slot_ref, w_ref, in_v, out_v, w_v, route_v, slot_v, sems):
    tok_rows, depth = tok_ref.shape
    route_load = start(route_ref, route_v, sems.at[9])
    width = wq_ref.shape[1]
    weight_loads = [
        start(wq_ref, w_v.at[:, :width], sems.at[6]),
        start(wv_ref, w_v.at[:, width:], sems.at[7]),
    ]
    loads = [
        start(tok_ref, in_v.at[:, :depth], sems.at[0]),
        start(cot_ref, in_v.at[:, depth:], sems.at[1]),
    ]
    route_load.wait()
    route = route_v[...]
    member = iota((OWNERS, tok_rows), 0) == route
    earlier = (iota((tok_rows, tok_rows), 0) < iota((tok_rows, tok_rows), 1)).astype(BF16)
    before = mm(member.astype(BF16), earlier)
    rank = jnp.sum(jnp.where(member, before, 0.0), axis=0, keepdims=True)
    slot = route * SLOT + rank.astype(jnp.int32)
    slot_v[...] = slot
    for c in weight_loads:
        c.wait()
    stores = [start(w_v, w_ref, sems.at[8]), start(slot_v, slot_ref, sems.at[10])]
    for c in loads:
        c.wait()
    step = 192
    for n in range(SLOTS // step):
        at = n * step
        row = iota((step, tok_rows), 0) + at
        pick = (row == slot).astype(BF16)
        count = jnp.sum((row == route * SLOT + (SLOT - 1)).astype(F32), axis=1, keepdims=True)
        out_v[at : at + step] = (mm(pick, in_v[...]) + count).astype(BF16)
        stores.append(start(out_v.at[at : at + step], out_ref.at[at : at + step], sems.at[2 + n]))
    for c in stores:
        c.wait()


def load_weights(ids_ref, block_refs, w_ref, sems):
    rows = block_refs[0].shape[0]
    z = ids_ref[0]
    c = ids_ref[1]
    copies = []
    for n, block in enumerate(block_refs):
        zb = lax.rem(z + (n % 8), 8)
        fb = 2 * zb + (c if n < 8 else 1 - c)
        copies.append(
            start(block, w_ref.at[pl.ds(pl.multiple_of(fb * rows, rows), rows)], sems.at[n])
        )
    return copies


def masked(scores, lo):
    width = scores.shape[1]
    eye = iota((width, width), 0) == iota((width, width), 1)
    parts = [jnp.where(eye, -1e30, scores[lo : lo + width])]
    if lo:
        parts.insert(0, scores[:lo])
    if lo + width < scores.shape[0]:
        parts.append(scores[lo + width :])
    return jnp.concatenate(parts, axis=0) if len(parts) > 1 else parts[0]


def blocks_of(members):
    return [(lo, min(lo + 128, members)) for lo in range(0, members, 128)]


def positions(rx_ref):
    pick = (iota((OWNERS, SLOTS), 1) == iota((OWNERS, SLOTS), 0) * SLOT + (SLOT - 1)).astype(BF16)
    count = mm(pick, rx_ref[:, 0:128])
    count_t = jnp.transpose(count)[0:8].astype(BF16)
    col = iota((OWNERS, SLOTS), 1)
    first = iota((OWNERS, SLOTS), 0) * SLOT
    past = (col >= first + SLOT).astype(F32)
    inside = ((col >= first) & (col < first + SLOT)).astype(BF16)
    offset = mm(count_t, past.astype(BF16))
    mine = mm(count_t, inside)
    within = iota((8, SLOTS), 1).astype(F32) - SLOT * jnp.sum(past, axis=0, keepdims=True)
    return jnp.where(within < mine, offset + within, -1.0)


def cluster_body(ids_hbm, rx_ref, *refs):
    block_refs = refs[:16]
    out_ref, gqv_ref, keep_ref, send_ref = refs[16:20]
    rx_v, w_v, xg_v, xt_v, qv_v, att_v, gqv_v, p_v, d_v, out_v, ids_ref, sems = refs[20:]
    members = xg_v.shape[0]
    depth = xt_v.shape[0]
    width = qv_v.shape[1] // 2
    heads = width // HEAD_DIM
    scaling = HEAD_DIM ** (-0.5)
    factor = scaling * LOG2E
    parts = [slice(0, HEAD_DIM), slice(HEAD_DIM, width)]
    parts += [slice(at, at + width) for at in range(width, depth + width, width)]
    loads = [start(rx_ref.at[:, p], rx_v.at[:, p], sems.at[18 + n]) for n, p in enumerate(parts)]
    start(ids_hbm, ids_ref, sems.at[40]).wait()
    weight_copies = load_weights(ids_ref, block_refs, w_v, sems)
    loads[0].wait()
    pos = positions(rx_v)
    comp = (iota((members, SLOTS), 0) == pos[0:1].astype(jnp.int32)).astype(BF16)
    loads[1].wait()
    for at in range(0, depth + width, width):
        if at:
            loads[1 + at // width].wait()
        xg_v[:, at : at + width] = mm(comp, rx_v[:, at : at + width]).astype(BF16)
    xt_v[:, :members] = jnp.transpose(xg_v[:, :depth])
    xt_v[:, members:] = jnp.zeros((depth, xt_v.shape[1] - members), BF16)
    rows = block_refs[0].shape[0]
    shares = []
    for n in range(8):
        to = slice(n * rows, (n + 1) * rows)
        for k, (core, target) in enumerate(((ids_ref[1], keep_ref), (1 - ids_ref[1], send_ref))):
            at = pl.multiple_of((2 * n + core) * rows, rows)
            shares.append(start(xt_v.at[pl.ds(at, rows)], target.at[to], sems.at[24 + 2 * n + k]))
    for c in weight_copies:
        c.wait()
    for at in (0, width):
        qv_v[:, at : at + width] = mm(xg_v[:, :depth], w_v[:, at : at + width]).astype(BF16)

    def head(h):
        at = h * HEAD_DIM
        at_v = width + at
        q = qv_v[:, pl.ds(at, HEAD_DIM)]
        v = qv_v[:, pl.ds(at_v, HEAD_DIM)]
        g = xg_v[:, pl.ds(depth + at, HEAD_DIM)]
        for lo, hi in blocks_of(members):
            scores = masked(mm(q, q[lo:hi], NT), lo)
            top = jnp.max(scores, axis=0, keepdims=True)
            weights = jnp.exp2((scores - top) * factor)
            probs = weights * (1.0 / jnp.sum(weights, axis=0, keepdims=True))
            p_v[:, lo:hi] = probs.astype(BF16)
            grad_probs = mm(v, g[lo:hi], NT)
            row_terms = jnp.sum(probs * grad_probs, axis=0, keepdims=True)
            d_v[:, lo:hi] = (probs * (grad_probs - row_terms) * scaling).astype(BF16)
        probs = p_v[...]
        grad_scores = d_v[...]
        att_v[:, pl.ds(at, HEAD_DIM)] = jnp.transpose(mm(jnp.transpose(v), probs)).astype(BF16)
        gqv_v[:, pl.ds(at_v, HEAD_DIM)] = mm(probs, g).astype(BF16)
        grad_q = mm(grad_scores, q) + jnp.transpose(mm(jnp.transpose(q), grad_scores))
        gqv_v[:, pl.ds(at, HEAD_DIM)] = grad_q.astype(BF16)

    for h in range(heads):
        head(h)
    gqv_copy = start(gqv_v, gqv_ref, sems.at[23])
    spread = (iota((SLOTS, members), 1) == column(pos[0:1])).astype(BF16)
    out_v[:, :width] = mm(spread, att_v[...]).astype(BF16)
    stores = [start(out_v.at[:, :width], out_ref.at[:, :width], sems.at[22])]
    for at in range(0, depth, width):
        grad = mm(gqv_v[...], w_v[at : at + width], NT).astype(BF16)
        to = slice(width + at, 2 * width + at)
        out_v[:, to] = mm(spread, grad).astype(BF16)
        stores.append(start(out_v.at[:, to], out_ref.at[:, to], sems.at[16 + at // width]))
    gqv_copy.wait()
    for c in shares + stores:
        c.wait()


def weight_grad_body(ids_hbm, *refs):
    ins, outs, ins_v, full_v, ids_ref, sems = refs[:4], refs[4:7], refs[7:11], refs[11], refs[12], refs[13]
    copies = [start(r, v, sems.at[n]) for n, (r, v) in enumerate(zip(ins, ins_v))]
    copies.append(start(ids_hbm, ids_ref, sems.at[20]))
    keep_v, own_v, xs_v, got_v = ins_v
    keep_ref, a_ref, b_ref = outs
    width = a_ref.shape[1]
    rows = a_ref.shape[0] // 4
    members = own_v.shape[0]
    for c in copies:
        c.wait()
    parity = lax.rem(ids_ref[0], 2)
    stores = []
    for half in (0, 1):
        cols = slice(half * width, (half + 1) * width)
        full_v[:, cols] = (mm(keep_v[:, :members], own_v[:, cols]) + mm(xs_v[:, :members], got_v[:, cols])).astype(BF16)
        for n in range(4):
            to = slice(n * rows, (n + 1) * rows)
            mine = pl.multiple_of((2 * n + parity) * rows, rows)
            other = pl.multiple_of((2 * n + 1 - parity) * rows, rows)
            at = 4 + 8 * half + 2 * n
            stores.append(
                start(full_v.at[pl.ds(mine, rows), cols], keep_ref.at[to, cols], sems.at[at])
            )
            stores.append(
                start(full_v.at[pl.ds(other, rows), cols], (a_ref, b_ref)[half].at[to], sems.at[at + 1])
            )
    for c in stores:
        c.wait()


def pair_sum_body(ids_ref, keep_ref, a_ref, b_ref, *refs):
    outs, total_ref = refs[:3], refs[3]
    width = a_ref.shape[1]
    rows = outs[0].shape[0] // 2
    total_ref[:, :width] = (keep_ref[:, :width].astype(F32) + a_ref[...].astype(F32)).astype(BF16)
    total_ref[:, width:] = (keep_ref[:, width:].astype(F32) + b_ref[...].astype(F32)).astype(BF16)
    bit = lax.rem(lax.div(ids_ref[0], 2), 2)
    for n in range(2):
        to = slice(n * rows, (n + 1) * rows)
        mine = pl.ds(pl.multiple_of((2 * n + bit) * rows, rows), rows)
        other = pl.ds(pl.multiple_of((2 * n + 1 - bit) * rows, rows), rows)
        outs[0][to] = total_ref[mine]
        outs[1][to] = total_ref[other, :width]
        outs[2][to] = total_ref[other, width:]


def quad_sum_body(keep_ref, a_ref, b_ref, out_ref):
    width = a_ref.shape[1]
    tall = out_ref.shape[1]
    low = tall // 3
    cols = width // OWNERS
    spare = out_ref.shape[2] - 2 * cols
    q = (keep_ref[:, :width].astype(F32) + a_ref[...].astype(F32)).astype(BF16)
    v = (keep_ref[:, width:].astype(F32) + b_ref[...].astype(F32)).astype(BF16)
    for n in range(OWNERS):
        qn = q[:, n * cols : (n + 1) * cols]
        vn = v[:, n * cols : (n + 1) * cols]
        out_ref[n, :, :cols] = qn[:tall]
        out_ref[n, :, cols : 2 * cols] = vn[:tall]
        rest = jnp.concatenate([qn[tall:], vn[tall:]], axis=1)
        for k in range(3):
            out_ref[n, k * low : (k + 1) * low, 2 * cols :] = rest[:, k * spare : (k + 1) * spare]


def seq_sum_body(ids_ref, in_ref, keep_ref, send_ref):
    total = in_ref[0].astype(F32)
    for n in range(1, OWNERS):
        total = total + in_ref[n].astype(F32)
    rows, cols = keep_ref.shape
    tall = total.shape[0]
    rest = total[:, cols:]
    third = tall // 3
    rest = jnp.concatenate([rest[k * third : (k + 1) * third] for k in range(3)], axis=1)
    total = jnp.concatenate([total[:, :cols], rest], axis=0)
    low = ids_ref[0] < 4
    keep_ref[...] = jnp.where(low, total[:rows], total[rows:])
    send_ref[...] = jnp.where(low, total[rows:], total[:rows])


def last_sum_body(keep_ref, got_ref, q_ref, v_ref):
    total = jnp.transpose(keep_ref[...] + got_ref[...])
    cols = q_ref.shape[0]
    q_ref[...] = total[:cols]
    v_ref[...] = total[cols:]


def unpack_body(slot_ref, back_ref, out_ref, slot_v, back_v, out_v, sems):
    tok_rows, wide = out_ref.shape
    step = wide // 2
    first = 0 if 3 * wide == back_ref.shape[1] else back_ref.shape[1] - wide
    slot_load = start(slot_ref, slot_v, sems.at[4])
    loads = [
        start(back_ref.at[:, first + n * step : first + (n + 1) * step], back_v.at[:, n * step : (n + 1) * step], sems.at[n])
        for n in range(2)
    ]
    slot_load.wait()
    pick = (iota((tok_rows, SLOTS), 1) == column(slot_v[...])).astype(BF16)
    stores = []
    for n in range(2):
        part = slice(n * step, (n + 1) * step)
        loads[n].wait()
        out_v[:, part] = mm(pick, back_v[:, part]).astype(BF16)
        stores.append(start(out_v.at[:, part], out_ref.at[:, part], sems.at[2 + n]))
    for c in stores:
        c.wait()


def z_shift(d):
    return [(2 * z + c, (z + d) % 8 * 2 + c) for z in range(8) for c in range(2)]


def z_pair(odd):
    return [
        (2 * z + c, ((z ^ 1) if not odd else (z + 1 if z % 2 else z - 1) % 8) * 2 + c)
        for z in range(8)
        for c in range(2)
    ]


def z_two(odd):
    return [
        (2 * z + c, (z + (2 if (z % 4 < 2) != bool(odd) else -2)) % 8 * 2 + c)
        for z in range(8)
        for c in range(2)
    ]


CORES = [(n, n ^ 1) for n in range(16)]


def to_core(data):
    return lax.ppermute(data, "fsdp", CORES)


def spread_slots(data):
    width = data.shape[1]
    out = lax.all_to_all(
        data.reshape(OWNERS, SLOT, width), "seq", split_axis=0, concat_axis=0, tiled=True
    )
    return out.reshape(SLOTS, width)


def gather_weights(block):
    own = [None] * 8
    own[0] = block
    up = down = block
    for step in range(1, 5):
        up = lax.ppermute(up, "fsdp", z_shift(1))
        own[8 - step] = up
        if step < 4:
            down = lax.ppermute(down, "fsdp", z_shift(7))
            own[step] = down
    return own + [to_core(b) for b in own]


def on_device(tokens, assignment, w_query, w_value, out_grad):
    features = tokens[0]
    cotangent = out_grad[0]
    tok_rows, depth = features.shape
    width = w_query.shape[1]
    members = tok_rows
    f = lax.axis_index("fsdp")
    ids = jnp.stack([f // 2, f % 2]).astype(jnp.int32)
    both = depth + width
    padded = -(-members // 128) * 128
    sems = pltpu.SemaphoreType.DMA
    packed, slot, block = pl.pallas_call(
        pack_body,
        out_shape=[
            jax.ShapeDtypeStruct((SLOTS, both), BF16),
            jax.ShapeDtypeStruct((1, tok_rows), jnp.int32),
            jax.ShapeDtypeStruct((depth // 16, 2 * width), BF16),
        ],
        in_specs=[hbm()] * 5,
        out_specs=[hbm()] * 3,
        scratch_shapes=[
            pltpu.VMEM((tok_rows, both), BF16),
            pltpu.VMEM((SLOTS, both), BF16),
            pltpu.VMEM((depth // 16, 2 * width), BF16),
            pltpu.VMEM((1, tok_rows), jnp.int32),
            pltpu.VMEM((1, tok_rows), jnp.int32),
            sems((11,)),
        ],
        compiler_params=pltpu.CompilerParams(vmem_limit_bytes=60 * MIB),
        cost_estimate=pl.CostEstimate(
            flops=2 * SLOTS * tok_rows * both, bytes_accessed=2 * (SLOTS + tok_rows) * both, transcendentals=0
        ),
    )(assignment, features, cotangent, w_query, w_value)
    blocks = gather_weights(block)
    received = spread_slots(packed)
    result, gqv, keep, send = call(
        cluster_body,
        [
            ((SLOTS, both), BF16),
            ((members, 2 * width), BF16),
            ((depth // 2, padded), BF16),
            ((depth // 2, padded), BF16),
        ],
        [hbm()] * 18,
        (ids, received, *blocks),
        out_space=hbm,
        scratch=[
            pltpu.VMEM((SLOTS, both), BF16),
            pltpu.VMEM((depth, 2 * width), BF16),
            pltpu.VMEM((members, both), BF16),
            pltpu.VMEM((depth, padded), BF16),
            pltpu.VMEM((members, 2 * width), BF16),
            pltpu.VMEM((members, width), BF16),
            pltpu.VMEM((members, 2 * width), BF16),
            pltpu.VMEM((members, members), BF16),
            pltpu.VMEM((members, members), BF16),
            pltpu.VMEM((SLOTS, both), BF16),
            pltpu.SMEM((2,), jnp.int32),
            sems((41,)),
        ],
        limit=50,
        flops=16 * 10**9,
        moved=20 * 10**6,
    )
    xs = to_core(send)
    got = to_core(gqv)
    back = spread_slots(result)
    rows = depth // 16
    keep, part_a, part_b = call(
        weight_grad_body,
        [((4 * rows, 2 * width), BF16), ((4 * rows, width), BF16), ((4 * rows, width), BF16)],
        [hbm()] * 5,
        (ids, keep, gqv, xs, got),
        out_space=hbm,
        scratch=[
            pltpu.VMEM((depth // 2, padded), BF16),
            pltpu.VMEM((members, 2 * width), BF16),
            pltpu.VMEM((depth // 2, padded), BF16),
            pltpu.VMEM((members, 2 * width), BF16),
            pltpu.VMEM((depth // 2, 2 * width), BF16),
            pltpu.SMEM((2,), jnp.int32),
            sems((21,)),
        ],
        limit=40,
        flops=3 * 10**9,
        moved=8 * 10**6,
    )
    part_a = lax.ppermute(part_a, "fsdp", z_pair(0))
    part_b = lax.ppermute(part_b, "fsdp", z_pair(1))
    keep, part_a, part_b = call(
        pair_sum_body,
        [((2 * rows, 2 * width), BF16), ((2 * rows, width), BF16), ((2 * rows, width), BF16)],
        [smem()] + [vmem()] * 3,
        (ids, keep, part_a, part_b),
        scratch=[pltpu.VMEM((4 * rows, 2 * width), BF16)],
        moved=4 * 10**6,
    )
    part_a = lax.ppermute(part_a, "fsdp", z_two(0))
    part_b = lax.ppermute(part_b, "fsdp", z_two(1))
    (last,) = call(
        quad_sum_body,
        [((OWNERS, rows * width // 512, 128), BF16)],
        [vmem()] * 3,
        (keep, part_a, part_b),
        moved=2 * 10**6,
    )
    last, back = lax.optimization_barrier((last, back))
    last = lax.all_to_all(last, "seq", split_axis=0, concat_axis=0, tiled=True)

    def unpack(wide, back):
        return call(
            unpack_body,
            [((tok_rows, wide), BF16)],
            [hbm()] * 2,
            (slot, back),
            out_space=hbm,
            scratch=[
                pltpu.VMEM((1, tok_rows), jnp.int32),
                pltpu.VMEM((SLOTS, wide), BF16),
                pltpu.VMEM((tok_rows, wide), BF16),
                sems((5,)),
            ],
            limit=60,
            flops=2 * SLOTS * tok_rows * wide,
            moved=2 * (SLOTS + tok_rows) * wide,
        )[0]

    attended = unpack(width, back)
    last, attended = lax.optimization_barrier((last, attended))
    keep, send = call(
        seq_sum_body,
        [((rows, width // 8), F32)] * 2,
        [smem(), vmem()],
        (ids, last),
        moved=10**6,
    )
    got = lax.ppermute(send, "fsdp", z_shift(4))
    grad_wq, grad_wv = call(
        last_sum_body, [((width // 16, rows), F32)] * 2, [vmem()] * 2, (keep, got), moved=10**5
    )
    back, grad_wq, grad_wv = lax.optimization_barrier((back, grad_wq, grad_wv))
    token_grad = unpack(depth, back)
    return attended[None], token_grad[None], grad_wq.T, grad_wv.T


def solution(mesh):
    in_specs = (
        P("fsdp", "seq", None),
        P("fsdp", "seq"),
        P("fsdp", None),
        P("fsdp", None),
        P("fsdp", "seq", None),
    )
    out_specs = (P("fsdp", "seq", None), P("fsdp", "seq", None), P("fsdp", "seq"), P("fsdp", "seq"))
    return jax.shard_map(
        on_device, mesh=mesh, in_specs=in_specs, out_specs=out_specs, check_vma=False
    )
```
